32 devices in a mesh: bz: 8 (over y, x, core), bxy: 4 (over z).
Axes of the slice: x: 2, y: 2, z: 4, core: 2. Of those that a mesh axis runs over, the one named last changes fastest.
Arguments:
- estimate: float32 [64, 64, 512], P('bz', 'bxy'), may hold values from 0.5 to 2
- observed: bfloat16 [3, 64, 64, 512], P(None, 'bz', 'bxy'), may hold values from 0.5 to 2
- psf_taps: float32 [3, 3, 3, 9], replicated, may hold values from 0.05 to 1
- view_shift: int32 [3], replicated, may hold values from 0 to 511
- intersection: int32 [3, 8, 4], replicated, may hold values 0 or 1
Outputs:
- updated: float32 [64, 64, 512], P('bz', 'bxy')
The draws below stay inside these ranges and needn't reach their ends.
All inputs are finite; a program needn't handle non-finite values.
Results may differ from the reference program's by a relative error of at most 0.0004.
Values may be sent and summed in bfloat16 or wider, within the bound.
A program may use at most 64 MiB of HBM per device.

```python
import math
import jax
import jax.numpy as jnp
from jax import lax

CZ = 8
CX = 16
NY = 512
VIEWS = 3
RANK = 3
RADIUS = 4
PASSES = 8
TAPS = 9
NZ = 64
NX = 64
BRICKS_Z = 8
BRICKS_X = 4


def touch_ends(array, key, smallest, largest):
    spot = [jax.random.randint(jax.random.fold_in(key, axis), (), 0, length) for axis, length in enumerate(array.shape)]
    widest = array.shape.index(max(array.shape))
    neighbour = spot[:widest] + [(spot[widest] + 1) % array.shape[widest]] + spot[widest + 1:]
    return array.at[tuple(spot)].set(smallest).at[tuple(neighbour)].set(largest)


def steps_of(stream_key, extent, shards, least, largest):
    factor_of = 1.0
    for axis_at, parts in shards:
        heights = jax.random.uniform(jax.random.fold_in(jax.random.fold_in(stream_key, 6), axis_at), (parts,), jnp.float32, least / len(shards), largest / len(shards))
        factor_of = factor_of * jnp.repeat(jnp.exp(heights), extent[axis_at] // parts).reshape((-1,) + (1,) * (len(extent) - 1 - axis_at))
    return factor_of


def setup_inputs(seed: int = 0) -> dict:
    key_of = jax.random.split(jax.random.key(seed), 6)
    estimate = jnp.clip(0.5 + 1.5 * jax.random.uniform(key_of[0], (NZ, NX, NY), jnp.float32) ** steps_of(key_of[0], (NZ, NX, NY), ((0, 8), (1, 4)), -0.2, 0.2), 0.5, 2.0)
    observed = jnp.clip(0.5 + 1.5 * jax.random.uniform(key_of[1], (VIEWS, NZ, NX, NY), jnp.float32) ** steps_of(key_of[1], (VIEWS, NZ, NX, NY), ((1, 8), (2, 4)), -0.2, 0.2), 0.5, 2.0).astype(jnp.bfloat16)
    psf_taps = jnp.clip(jnp.exp(jax.random.uniform(key_of[2], (VIEWS, RANK, 3, TAPS), jnp.float32, math.log(0.05), math.log(1.0))), 0.05, 1.0)
    view_shift = jax.random.randint(key_of[3], (VIEWS,), 0, NY).astype(jnp.int32)
    intersection = touch_ends((jax.random.randint(key_of[4], (VIEWS, BRICKS_Z, BRICKS_X), 0, 4) < 3).astype(jnp.int32), jax.random.fold_in(key_of[4], 1), 0, 1)
    return {"estimate": estimate, "observed": observed, "psf_taps": psf_taps, "view_shift": view_shift, "intersection": intersection}


EPS_TV = 0.25
TAU = 0.08
BACKGROUND = 0.1

def tv_pass(field):
    padded = jnp.pad(field, 1, mode='edge')
    beside_list = (padded[:-2, 1:-1, 1:-1], padded[2:, 1:-1, 1:-1], padded[1:-1, :-2, 1:-1], padded[1:-1, 2:, 1:-1], padded[1:-1, 1:-1, :-2], padded[1:-1, 1:-1, 2:])
    total = jnp.zeros_like(field)
    for beside in beside_list:
        diff = beside - field
        total = total + diff / jnp.sqrt(diff * diff + EPS_TV)
    return field + TAU * total

def conv_valid(values, kernel, axis):
    length = values.shape[axis] - (kernel.shape[0] - 1)
    total = kernel[0] * lax.slice_in_dim(values, 0, length, axis=axis)
    for tap in range(1, kernel.shape[0]):
        total = total + kernel[tap] * lax.slice_in_dim(values, tap, tap + length, axis=axis)
    return total

def conv_full(values, kernel, axis):
    widths = [(0, 0)] * 3
    widths[axis] = (RADIUS, RADIUS)
    return conv_valid(jnp.pad(values, widths), kernel, axis)

def reference(estimate, observed, psf_taps, view_shift, intersection):
    smoothed = estimate
    for pass_index in range(PASSES):
        smoothed = tv_pass(smoothed)
    sent = lax.optimization_barrier(smoothed.astype(jnp.bfloat16))
    sent_full = sent.astype(jnp.float32)
    kernels = psf_taps / lax.optimization_barrier(jnp.sum(psf_taps, axis=-1, keepdims=True))
    cell_mask = jnp.repeat(jnp.repeat(intersection, CZ, axis=1), CX, axis=2)
    correction = jnp.zeros(estimate.shape, jnp.float32)
    for view in range(VIEWS):
        moved = jnp.roll(sent_full, view_shift[view], axis=2)
        image = jnp.zeros(estimate.shape, jnp.float32)
        for rank_index in range(RANK):
            blurred = conv_full(moved, kernels[view, rank_index, 2], 2)
            blurred = conv_full(blurred, kernels[view, rank_index, 1], 1)
            blurred = conv_full(blurred, kernels[view, rank_index, 0], 0)
            image = image + blurred
        image = image / RANK
        ratio = jnp.where(cell_mask[view][:, :, None] > 0, observed[view].astype(jnp.float32) / (image + BACKGROUND), 1.0)
        ratio = lax.optimization_barrier(ratio.astype(jnp.bfloat16)).astype(jnp.float32)
        back = jnp.zeros(estimate.shape, jnp.float32)
        for rank_index in range(RANK):
            spread = conv_full(ratio, kernels[view, rank_index, 0][::-1], 0)
            spread = conv_full(spread, kernels[view, rank_index, 1][::-1], 1)
            spread = conv_full(spread, kernels[view, rank_index, 2][::-1], 2)
            back = back + spread
        back = back / RANK
        correction = correction + jnp.roll(back, -view_shift[view], axis=2)
    return smoothed * correction / VIEWS
```

```python
import functools

import jax
import jax.numpy as jnp
import numpy as np
from jax import lax
from jax.experimental import pallas as pl
from jax.experimental.pallas import tpu as pltpu

VIEWS = 3
RANK = 3
RADIUS = 4
TAPS = 9
PASSES = 8
EPS_TV = 0.25
TAU = 0.08
BACKGROUND = 0.1
CZ, CX = 8, 16
ROWS = CZ * CX
FULL = (CZ + 2 * RADIUS) * (CX + 2 * RADIUS)
DIRS = [(-1, 0), (1, 0), (0, -1), (0, 1), (-1, -1), (-1, 1), (1, -1), (1, 1)]
BF = jnp.bfloat16
F32 = jnp.float32
SPOT = {
    (-1, 0): (128, 64),
    (1, 0): (192, 64),
    (0, -1): (256, 32),
    (0, 1): (288, 32),
    (-1, -1): (320, 16),
    (-1, 1): (336, 16),
    (1, -1): (352, 16),
    (1, 1): (368, 16),
}


def row_places():
    z = np.zeros(FULL, np.int32)
    x = np.zeros(FULL, np.int32)
    z_of = {-1: range(-RADIUS, 0), 0: range(CZ), 1: range(CZ, CZ + RADIUS)}
    x_of = {-1: range(-RADIUS, 0), 0: range(CX), 1: range(CX, CX + RADIUS)}
    for (dz, dx), (first, _) in [((0, 0), (0, 0))] + list(SPOT.items()):
        at = first
        for zi in z_of[dz]:
            for xi in x_of[dx]:
                z[at], x[at] = zi, xi
                at += 1
    tap_z = z[None] - np.arange(CZ, dtype=np.int32)[:, None] + RADIUS
    tap_x = x[None] - np.arange(CX, dtype=np.int32)[:, None] + RADIUS
    return np.concatenate([tap_z, tap_x], axis=0)


def flux(diff):
    return diff * lax.rsqrt(diff * diff + EPS_TV)


def kernel(
    sizes, taps, shift, inter, est, obs, places, out,
    own1, strip1, got1, nat, u, pack, f2, x2, f3, x3, w_f, w_a, c_f, c_a, obs_r, tmp, img, corr,
    sems1, semr1, sems2, semr2, sems3, semr3,
):
    nz, nx = sizes
    iz, ix = lax.axis_index("bz"), lax.axis_index("bxy")
    ny = est.shape[2]

    def exists(d):
        dz, dx = d
        ok = None
        for step, at, count in ((dz, iz, nz), (dx, ix, nx)):
            if step:
                here = at > 0 if step < 0 else at < count - 1
                ok = here if ok is None else jnp.logical_and(ok, here)
        return ok

    def peer(d):
        return {"bz": iz + d[0], "bxy": ix + d[1]}

    def opposite(d):
        return (-d[0], -d[1])

    barrier = pltpu.get_barrier_semaphore()
    for d in DIRS:
        @pl.when(exists(d))
        def _():
            pl.semaphore_signal(barrier, inc=1, device_id=peer(d), device_id_type=pl.DeviceIdType.MESH)

    own1[...] = est[...].astype(BF)
    for side in range(2):
        part = est[:, 8 * side:8 * side + 8, :]
        strip1[side] = part.reshape(4, 16, ny).astype(BF)
    for n, d in enumerate(DIRS):
        @pl.when(jnp.logical_not(exists(d)))
        def _():
            got1[n] = jnp.zeros(got1.shape[1:], BF)
            first, rows = SPOT[d]
            zero = jnp.zeros((rows, ny), BF)
            f2[first:first + rows] = zero
            for v in range(VIEWS):
                f3[v, first:first + rows] = zero

    wide_z = 3 - jnp.where(iz == 0, 1, 0) - jnp.where(iz == nz - 1, 1, 0)
    wide_x = 3 - jnp.where(ix == 0, 1, 0) - jnp.where(ix == nx - 1, 1, 0)
    pl.semaphore_wait(barrier, wide_z * wide_x - 1)

    def round1(n):
        d = DIRS[n]
        there = DIRS.index(opposite(d))
        if d[1] == 0:
            src, dst = own1, got1.at[there]
        else:
            src, dst = strip1.at[0 if d[1] < 0 else 1], got1.at[there, 0:4]
        return pltpu.make_async_remote_copy(
            src_ref=src, dst_ref=dst, send_sem=sems1.at[n], recv_sem=semr1.at[n],
            device_id=peer(d), device_id_type=pl.DeviceIdType.MESH)

    def round23(n, field, strips, send_sem, recv_sem):
        d = DIRS[n]
        first, rows = SPOT[opposite(d)]
        if d[1] == 0:
            src = field.at[0:64] if d[0] < 0 else field.at[64:128]
        else:
            side = 0 if d[1] < 0 else 1
            low = 0 if d[0] <= 0 else 16
            src = strips.at[side, low:low + rows]
        return pltpu.make_async_remote_copy(
            src_ref=src, dst_ref=field.at[first:first + rows], send_sem=send_sem, recv_sem=recv_sem,
            device_id=peer(d), device_id_type=pl.DeviceIdType.MESH)

    def start(copy_of):
        for n, d in enumerate(DIRS):
            @pl.when(exists(d))
            def _():
                copy_of(n).start()

    def finish_send(copy_of):
        for n, d in enumerate(DIRS):
            @pl.when(exists(d))
            def _():
                copy_of(n).wait_send()

    def finish_recv(copy_of):
        for n, d in enumerate(DIRS):
            @pl.when(exists(opposite(d)))
            def _():
                copy_of(n).wait_recv()

    start(round1)

    lane = lax.broadcasted_iota(jnp.int32, (8, ny), 1)
    tap_z = places[0:CZ]
    tap_x = places[CZ:CZ + CX]

    def prepare(v, carry):
        moved = (lane + shift[v]) & (ny - 1)
        for r in range(RANK):
            sums = []
            for axis in range(3):
                base = ((v * RANK + r) * 3 + axis) * TAPS
                total = taps[base]
                for t in range(1, TAPS):
                    total = total + taps[base + t]
                sums.append(total)
            base = (v * RANK + r) * 3 * TAPS
            for w, forward in ((w_f, True), (w_a, False)):
                a = jnp.zeros((CZ, FULL), F32)
                b = jnp.zeros((CX, FULL), F32)
                for t in range(TAPS):
                    at = t if forward else TAPS - 1 - t
                    a = jnp.where(tap_z == t, taps[base + at], a)
                    b = jnp.where(tap_x == t, taps[base + TAPS + at], b)
                a = a / (sums[0] * RANK)
                b = b / sums[1]
                for zo in range(CZ):
                    whole = a[zo:zo + 1] * b
                    high = whole.astype(BF)
                    rows = pl.ds(r * ROWS + zo * CX, CX)
                    w[v, rows, 0:FULL] = high
                    w[v, rows, FULL:2 * FULL] = (whole - high.astype(F32)).astype(BF)
            scale = 1.0 / jnp.full((8, ny), sums[2], F32)
            for t in range(TAPS):
                value = scale * taps[base + 2 * TAPS + t]
                for c, place in ((c_f, moved - (t - RADIUS)), (c_a, moved + (t - RADIUS))):
                    inside = (place >= 0) & (place < ny)
                    c[v, r * TAPS + t] = jnp.where(inside, value, 0.0)
        back = (ny - shift[v]) & (ny - 1)
        for z in range(CZ):
            obs_r[v, z] = pltpu.roll(obs[v, z].astype(F32), back, 1)
        return carry

    lax.fori_loop(0, VIEWS, prepare, 0)

    finish_recv(round1)

    columns = range(ny // 128)
    for c in columns:
        at = slice(128 * c, 128 * c + 128)
        nat[8:16, c, 8:24] = est[:, :, at]
        nat[0:8, c, 8:24] = got1[0, :, :, at].astype(F32)
        nat[16:24, c, 8:24] = got1[1, :, :, at].astype(F32)
        for n, z0, x0 in ((2, 8, 0), (3, 8, 24), (4, 0, 0), (5, 0, 24), (6, 16, 0), (7, 16, 24)):
            nat[z0:z0 + 8, c, x0:x0 + 8] = got1[n, 0:4, :, at].astype(F32).reshape(8, 8, 128)

    def relayout(z, carry):
        for i in range(4):
            for c in columns:
                u[z, i, :, 128 * c:128 * c + 128] = nat[z, c, pl.ds(i, 8, stride=4), :]
        return carry

    lax.fori_loop(0, 24, relayout, 0)

    sub = lax.broadcasted_iota(jnp.int32, (8, 128), 0)
    low_x = jnp.where(ix == 0, 0.0, 1.0)
    high_x = jnp.where(ix == nx - 1, 0.0, 1.0)
    x_mask = jnp.where(sub == 1, low_x, jnp.where(sub == 5, high_x, 1.0))
    x_mask = jnp.concatenate([x_mask] * (ny // 128), axis=1)
    y_mask = jnp.where(lax.broadcasted_iota(jnp.int32, (8, 128), 1) == 127, 0.0, 1.0)

    def tv(p, carry):
        @pl.when(iz == 0)
        def _():
            u[7] = u[8]

        @pl.when(iz == nz - 1)
        def _():
            u[16] = u[15]

        def plane(z, below):
            here = [u[z, i] for i in range(4)]
            above = [flux(u[z + 1, i] - here[i]) for i in range(4)]
            fx = [flux(here[i + 1] - here[i]) for i in range(3)]
            fx.append(flux(pltpu.roll(here[0], 7, 0) - here[3]) * x_mask)
            fx_low = [pltpu.roll(fx[3], 1, 0)] + fx[:3]
            for i in range(4):
                fy = flux(pltpu.roll(here[i], ny - 1, 1) - here[i])
                fy = jnp.concatenate([fy[:, :ny - 128], fy[:, ny - 128:] * y_mask], axis=1)
                total = (above[i] - below[i]) + (fx[i] - fx_low[i]) + (fy - pltpu.roll(fy, 1, 1))
                u[z, i] = here[i] + TAU * total
            return tuple(above)

        first = tuple(flux(u[p, i] - u[p - 1, i]) for i in range(4))
        lax.fori_loop(p, 24 - p, plane, first)
        return carry

    lax.fori_loop(1, PASSES + 1, tv, 0)
    finish_send(round1)

    def natural(z, carry):
        for i in range(4):
            for c in columns:
                nat[z, c, pl.ds(i, 8, stride=4), :] = u[z, i, :, 128 * c:128 * c + 128]
        return carry

    lax.fori_loop(8, 16, natural, 0)

    def fill(field, strips, read):
        for z in range(CZ):
            field[z * CX:(z + 1) * CX] = read(z).astype(BF)
            pack[0, 4 * z:4 * z + 4] = read(z)[0:4]
            pack[1, 4 * z:4 * z + 4] = read(z)[12:16]
        strips[...] = pack[...].astype(BF)

    fill(f2, x2, lambda z: jnp.concatenate([nat[8 + z, c, 8:24] for c in columns], axis=1))
    round2 = lambda n: round23(n, f2, x2, sems2.at[n], semr2.at[n])
    start(round2)
    finish_recv(round2)

    f2d = jnp.concatenate([f2[0:FULL], f2[0:FULL]], axis=0)

    def along_y(c, v, j, sign):
        parts = [tmp[r, j] for r in range(RANK)]
        total = None
        for t in range(TAPS):
            term = c[v, t] * parts[0]
            for r in range(1, RANK):
                term = term + c[v, r * TAPS + t] * parts[r]
            move = (sign * (t - RADIUS)) % ny
            if move:
                term = pltpu.roll(term, move, 1)
            total = term if total is None else total + term
        return total

    def round3(v):
        return lambda n: round23(n, f3.at[v], x3.at[v], sems3.at[v, n], semr3.at[v, n])

    for v in range(VIEWS):
        tmp[...] = jnp.dot(w_f[v], f2d, preferred_element_type=F32).reshape(tmp.shape)
        flag = inter[(v * nz + iz) * nx + ix]

        def ratios(j, carry):
            image = along_y(c_f, v, j, -1)
            img[j] = jnp.where(flag > 0, obs_r[v, j // 2, pl.ds((j % 2) * 8, 8), :] / (image + BACKGROUND), 1.0)
            return carry

        lax.fori_loop(0, 16, ratios, 0)
        fill(f3.at[v], x3.at[v], lambda z: img[2 * z:2 * z + 2].reshape(CX, ny))
        start(round3(v))
    finish_send(round2)

    for v in range(VIEWS):
        finish_recv(round3(v))
        f3d = jnp.concatenate([f3[v], f3[v]], axis=0)
        tmp[...] = jnp.dot(w_a[v], f3d, preferred_element_type=F32).reshape(tmp.shape)

        def spread(j, carry):
            back = along_y(c_a, v, j, 1)
            if v:
                back = back + corr[j]
            if v < VIEWS - 1:
                corr[j] = back
            else:
                z, x = j // 2, (j % 2) * 8
                smoothed = jnp.concatenate([nat[8 + z, c, pl.ds(8 + x, 8)] for c in columns], axis=1)
                out[z, pl.ds(x, 8), :] = smoothed * back / VIEWS
            return carry

        lax.fori_loop(0, 16, spread, 0)
    for v in range(VIEWS):
        finish_send(round3(v))


def local(sizes, estimate, observed, psf_taps, view_shift, intersection):
    cz, cx, ny = estimate.shape
    places = jnp.asarray(row_places())
    vmem = pl.BlockSpec(memory_space=pltpu.VMEM)
    smem = pl.BlockSpec(memory_space=pltpu.SMEM)
    dma = pltpu.SemaphoreType.DMA
    return pl.pallas_call(
        functools.partial(kernel, sizes),
        out_shape=jax.ShapeDtypeStruct((cz, cx, ny), F32),
        in_specs=[smem, smem, smem, vmem, vmem, vmem],
        out_specs=vmem,
        scratch_shapes=[
            pltpu.VMEM((cz, cx, ny), BF),
            pltpu.VMEM((2, 4, 16, ny), BF),
            pltpu.VMEM((8, 8, 16, ny), BF),
            pltpu.VMEM((24, ny // 128, 32, 128), F32),
            pltpu.VMEM((24, 4, 8, ny), F32),
            pltpu.VMEM((2, 32, ny), F32),
            pltpu.VMEM((FULL, ny), BF),
            pltpu.VMEM((2, 32, ny), BF),
            pltpu.VMEM((VIEWS, FULL, ny), BF),
            pltpu.VMEM((VIEWS, 2, 32, ny), BF),
            pltpu.VMEM((VIEWS, RANK * ROWS, 2 * FULL), BF),
            pltpu.VMEM((VIEWS, RANK * ROWS, 2 * FULL), BF),
            pltpu.VMEM((VIEWS, RANK * TAPS, 8, ny), F32),
            pltpu.VMEM((VIEWS, RANK * TAPS, 8, ny), F32),
            pltpu.VMEM((VIEWS, cz, cx, ny), F32),
            pltpu.VMEM((RANK, 16, 8, ny), F32),
            pltpu.VMEM((16, 8, ny), F32),
            pltpu.VMEM((16, 8, ny), F32),
            dma((8,)), dma((8,)), dma((8,)), dma((8,)), dma((VIEWS, 8)), dma((VIEWS, 8)),
        ],
        compiler_params=pltpu.CompilerParams(
            collective_id=0, has_side_effects=True, vmem_limit_bytes=56 * 1024 * 1024),
        cost_estimate=pl.CostEstimate(flops=10**9, bytes_accessed=10**6, transcendentals=5 * 10**6),
    )(psf_taps.reshape(-1), view_shift, intersection.reshape(-1), estimate, observed, places)


def solution(mesh):
    from jax.sharding import PartitionSpec as P
    sizes = (mesh.shape["bz"], mesh.shape["bxy"])
    return jax.shard_map(
        functools.partial(local, sizes),
        mesh=mesh,
        in_specs=(P("bz", "bxy", None), P(None, "bz", "bxy", None), P(), P(), P()),
        out_specs=P("bz", "bxy", None),
        check_vma=False,
    )
```

```python
import functools

import jax
import jax.numpy as jnp
import numpy as np
from jax import lax
from jax.experimental import pallas as pl
from jax.experimental.pallas import tpu as pltpu

VIEWS = 3
RANK = 3
RADIUS = 4
TAPS = 9
PASSES = 8
ROUNDS = 3 + VIEWS
EPS_TV = 0.25
TAU = 0.08
BACKGROUND = 0.1
CZ, CX = 8, 16
ROWS = CZ * CX
FULL = (CZ + 2 * RADIUS) * (CX + 2 * RADIUS)
DIRS = [(-1, 0), (1, 0), (0, -1), (0, 1), (-1, -1), (-1, 1), (1, -1), (1, 1)]
BF = jnp.bfloat16
F32 = jnp.float32
SPOT = {
    (-1, 0): (128, 64),
    (1, 0): (192, 64),
    (0, -1): (256, 32),
    (0, 1): (288, 32),
    (-1, -1): (320, 16),
    (-1, 1): (336, 16),
    (1, -1): (352, 16),
    (1, 1): (368, 16),
}


def row_places():
    z = np.zeros(FULL, np.int32)
    x = np.zeros(FULL, np.int32)
    z_of = {-1: range(-RADIUS, 0), 0: range(CZ), 1: range(CZ, CZ + RADIUS)}
    x_of = {-1: range(-RADIUS, 0), 0: range(CX), 1: range(CX, CX + RADIUS)}
    for (dz, dx), (first, _) in [((0, 0), (0, 0))] + list(SPOT.items()):
        at = first
        for zi in z_of[dz]:
            for xi in x_of[dx]:
                z[at], x[at] = zi, xi
                at += 1
    tap_z = z[None] - np.arange(CZ, dtype=np.int32)[:, None] + RADIUS
    tap_x = x[None] - np.arange(CX, dtype=np.int32)[:, None] + RADIUS
    return np.concatenate([tap_z, tap_x], axis=0)


def flux(diff):
    return diff * lax.rsqrt(diff * diff + EPS_TV)


def kernel(
    sizes, taps, shift, inter, est, obs, places, out,
    nat, u, pack, fields, strips, w_f, w_a, c_f, c_a, obs_r, tmp, img, corr, send_sems, recv_sems,
):
    nz, nx = sizes
    iz, ix = lax.axis_index("bz"), lax.axis_index("bxy")
    ny = est.shape[2]

    def exists(d):
        dz, dx = d
        ok = None
        for step, at, count in ((dz, iz, nz), (dx, ix, nx)):
            if step:
                here = at > 0 if step < 0 else at < count - 1
                ok = here if ok is None else jnp.logical_and(ok, here)
        return ok

    def peer(d):
        return {"bz": iz + d[0], "bxy": ix + d[1]}

    def opposite(d):
        return (-d[0], -d[1])

    barrier = pltpu.get_barrier_semaphore()
    for d in DIRS:
        @pl.when(exists(d))
        def _():
            pl.semaphore_signal(barrier, inc=1, device_id=peer(d), device_id_type=pl.DeviceIdType.MESH)

    for d in DIRS:
        @pl.when(jnp.logical_not(exists(d)))
        def _():
            first, rows = SPOT[d]
            for k in range(ROUNDS):
                fields[k, first:first + rows] = jnp.zeros((rows, ny), BF)

    def fill(k, read):
        for z in range(CZ):
            fields[k, z * CX:(z + 1) * CX] = read(z).astype(BF)
            pack[0, 4 * z:4 * z + 4] = read(z)[0:4]
            pack[1, 4 * z:4 * z + 4] = read(z)[12:16]
        strips[k] = pack[...].astype(BF)

    fill(0, lambda z: est[z])

    wide_z = 3 - jnp.where(iz == 0, 1, 0) - jnp.where(iz == nz - 1, 1, 0)
    wide_x = 3 - jnp.where(ix == 0, 1, 0) - jnp.where(ix == nx - 1, 1, 0)
    pl.semaphore_wait(barrier, wide_z * wide_x - 1)

    def copy_of(k, n):
        d = DIRS[n]
        first, rows = SPOT[opposite(d)]
        if d[1] == 0:
            low = 0 if d[0] < 0 else 64
            src = fields.at[k, low:low + 64]
        else:
            side = 0 if d[1] < 0 else 1
            low = 0 if d[0] <= 0 else 16
            src = strips.at[k, side, low:low + rows]
        return pltpu.make_async_remote_copy(
            src_ref=src, dst_ref=fields.at[k, first:first + rows],
            send_sem=send_sems.at[k, n], recv_sem=recv_sems.at[k, n],
            device_id=peer(d), device_id_type=pl.DeviceIdType.MESH)

    def start(k):
        for n, d in enumerate(DIRS):
            @pl.when(exists(d))
            def _():
                copy_of(k, n).start()

    def finish_send(k):
        for n, d in enumerate(DIRS):
            @pl.when(exists(d))
            def _():
                copy_of(k, n).wait_send()

    def finish_recv(k):
        for n, d in enumerate(DIRS):
            @pl.when(exists(opposite(d)))
            def _():
                copy_of(k, n).wait_recv()

    start(0)

    lane = lax.broadcasted_iota(jnp.int32, (8, ny), 1)
    tap_z = places[0:CZ]
    tap_x = places[CZ:CZ + CX]

    def prepare(v):
        moved = (lane + shift[v]) & (ny - 1)
        for r in range(RANK):
            sums = []
            for axis in range(3):
                total = taps[v, r, axis, 0]
                for t in range(1, TAPS):
                    total = total + taps[v, r, axis, t]
                sums.append(total)
            for w, forward in ((w_f, True), (w_a, False)):
                a = jnp.zeros((CZ, FULL), F32)
                b = jnp.zeros((CX, FULL), F32)
                for t in range(TAPS):
                    at = t if forward else TAPS - 1 - t
                    a = jnp.where(tap_z == t, taps[v, r, 0, at], a)
                    b = jnp.where(tap_x == t, taps[v, r, 1, at], b)
                a = a / (sums[0] * RANK)
                b = b / sums[1]
                for zo in range(CZ):
                    whole = a[zo:zo + 1] * b
                    high = whole.astype(BF)
                    rows = pl.ds(r * ROWS + zo * CX, CX)
                    w[v, rows, 0:FULL] = high
                    w[v, rows, FULL:2 * FULL] = (whole - high.astype(F32)).astype(BF)
            scale = 1.0 / jnp.full((8, ny), sums[2], F32)
            for t in range(TAPS):
                value = scale * taps[v, r, 2, t]
                for c, place in ((c_f, moved - (t - RADIUS)), (c_a, moved + (t - RADIUS))):
                    inside = (place >= 0) & (place < ny)
                    c[v, r * TAPS + t] = jnp.where(inside, value, 0.0)
        back = (ny - shift[v]) & (ny - 1)
        for z in range(CZ):
            obs_r[v, z] = pltpu.roll(obs[v, z].astype(F32), back, 1)

    prepare(0)
    finish_recv(0)

    columns = range(ny // 128)
    for c in columns:
        nat[4:12, c, 8:24] = est[:, :, 128 * c:128 * c + 128]

    def assemble(k):
        for c in columns:
            at = slice(128 * c, 128 * c + 128)
            for dz, dx in DIRS:
                first, rows = SPOT[(dz, dx)]
                piece = fields[k, first:first + rows, at].astype(F32)
                z0 = {-1: 0, 0: 4, 1: 12}[dz]
                if dx == 0:
                    nat[z0:z0 + 4, c, 8:24] = piece.reshape(4, 16, 128)
                else:
                    x0 = 4 if dx < 0 else 24
                    for z in range(rows // 4):
                        nat[z0 + z, c, x0:x0 + 4] = piece[4 * z:4 * z + 4]

        def relayout(z, carry):
            for i in range(3):
                for c in columns:
                    u[z, i, :, 128 * c:128 * c + 128] = nat[z, c, pl.ds(4 + i, 8, stride=3), :]
            return carry

        lax.fori_loop(0, 16, relayout, 0)

    sub = lax.broadcasted_iota(jnp.int32, (8, 128), 0)
    low_x = jnp.where(ix == 0, 0.0, 1.0)
    high_x = jnp.where(ix == nx - 1, 0.0, 1.0)
    masks = []
    for at, keep in ((1, low_x), (6, high_x)):
        masks.append(jnp.concatenate([jnp.where(sub == at, keep, 1.0)] * (ny // 128), axis=1))
    y_mask = jnp.where(lax.broadcasted_iota(jnp.int32, (8, 128), 1) == 127, 0.0, 1.0)

    def tv(p, carry):
        @pl.when(iz == 0)
        def _():
            u[3] = u[4]

        @pl.when(iz == nz - 1)
        def _():
            u[12] = u[11]

        def plane(z, below):
            here = [u[z, i] for i in range(3)]
            above = [flux(u[z + 1, i] - here[i]) for i in range(3)]
            fx = [flux(here[i + 1] - here[i]) * masks[i] for i in range(2)]
            fx.append(flux(pltpu.roll(here[0], 7, 0) - here[2]))
            fx_low = [pltpu.roll(fx[2], 1, 0)] + fx[:2]
            for i in range(3):
                fy = flux(pltpu.roll(here[i], ny - 1, 1) - here[i])
                fy = jnp.concatenate([fy[:, :ny - 128], fy[:, ny - 128:] * y_mask], axis=1)
                total = (above[i] - below[i]) + (fx[i] - fx_low[i]) + (fy - pltpu.roll(fy, 1, 1))
                u[z, i] = here[i] + TAU * total
            return tuple(above)

        first = tuple(flux(u[p, i] - u[p - 1, i]) for i in range(3))
        lax.fori_loop(p, 16 - p, plane, first)
        return carry

    def natural(z, carry):
        for i in range(3):
            for c in columns:
                nat[z, c, pl.ds(4 + i, 8, stride=3), :] = u[z, i, :, 128 * c:128 * c + 128]
        return carry

    for half in range(2):
        assemble(half)
        lax.fori_loop(1, PASSES // 2 + 1, tv, 0)
        lax.fori_loop(4, 12, natural, 0)
        fill(half + 1, lambda z: jnp.concatenate([nat[4 + z, c, 8:24] for c in columns], axis=1))
        start(half + 1)
        prepare(half + 1)
        finish_recv(half + 1)

    f2d = jnp.concatenate([fields[2], fields[2]], axis=0)

    def along_y(c, v, j, sign):
        parts = [tmp[r, pl.ds(2 * j, 2)] for r in range(RANK)]
        total = None
        for t in range(TAPS):
            term = c[v, t] * parts[0]
            for r in range(1, RANK):
                term = term + c[v, r * TAPS + t] * parts[r]
            move = (sign * (t - RADIUS)) % ny
            if move:
                term = pltpu.roll(term, move, 2)
            total = term if total is None else total + term
        return total

    for v in range(VIEWS):
        tmp[...] = jnp.dot(w_f[v], f2d, preferred_element_type=F32).reshape(tmp.shape)
        flag = inter[v, iz, ix]

        def ratios(j, carry):
            image = along_y(c_f, v, j, -1)
            img[j] = jnp.where(flag > 0, obs_r[v, j] / (image.reshape(CX, ny) + BACKGROUND), 1.0)
            return carry

        lax.fori_loop(0, CZ, ratios, 0)
        fill(3 + v, lambda z: img[z])
        start(3 + v)

    for v in range(VIEWS):
        finish_recv(3 + v)
        f3d = jnp.concatenate([fields[3 + v], fields[3 + v]], axis=0)
        tmp[...] = jnp.dot(w_a[v], f3d, preferred_element_type=F32).reshape(tmp.shape)

        def spread(j, carry):
            back = along_y(c_a, v, j, 1).reshape(CX, ny)
            if v:
                back = back + corr[j]
            if v < VIEWS - 1:
                corr[j] = back
            else:
                smoothed = jnp.concatenate([nat[4 + j, c, 8:24] for c in columns], axis=1)
                out[j] = smoothed * back / VIEWS
            return carry

        lax.fori_loop(0, CZ, spread, 0)
    for k in range(ROUNDS):
        finish_send(k)


def local(sizes, estimate, observed, psf_taps, view_shift, intersection):
    cz, cx, ny = estimate.shape
    places = jnp.asarray(row_places())
    vmem = pl.BlockSpec(memory_space=pltpu.VMEM)
    smem = pl.BlockSpec(memory_space=pltpu.SMEM)
    dma = pltpu.SemaphoreType.DMA
    return pl.pallas_call(
        functools.partial(kernel, sizes),
        out_shape=jax.ShapeDtypeStruct((cz, cx, ny), F32),
        in_specs=[smem, smem, smem, vmem, vmem, vmem],
        out_specs=vmem,
        scratch_shapes=[
            pltpu.VMEM((16, ny // 128, 32, 128), F32),
            pltpu.VMEM((16, 3, 8, ny), F32),
            pltpu.VMEM((2, 32, ny), F32),
            pltpu.VMEM((ROUNDS, FULL, ny), BF),
            pltpu.VMEM((ROUNDS, 2, 32, ny), BF),
            pltpu.VMEM((VIEWS, RANK * ROWS, 2 * FULL), BF),
            pltpu.VMEM((VIEWS, RANK * ROWS, 2 * FULL), BF),
            pltpu.VMEM((VIEWS, RANK * TAPS, 8, ny), F32),
            pltpu.VMEM((VIEWS, RANK * TAPS, 8, ny), F32),
            pltpu.VMEM((VIEWS, cz, cx, ny), F32),
            pltpu.VMEM((RANK, 16, 8, ny), F32),
            pltpu.VMEM((CZ, CX, ny), F32),
            pltpu.VMEM((CZ, CX, ny), F32),
            dma((ROUNDS, 8)), dma((ROUNDS, 8)),
        ],
        compiler_params=pltpu.CompilerParams(
            collective_id=0, has_side_effects=True, vmem_limit_bytes=24 * 1024 * 1024),
        cost_estimate=pl.CostEstimate(flops=10**9, bytes_accessed=10**6, transcendentals=5 * 10**6),
    )(psf_taps, view_shift, intersection, estimate, observed, places)


def solution(mesh):
    from jax.sharding import PartitionSpec as P
    sizes = (mesh.shape["bz"], mesh.shape["bxy"])
    return jax.shard_map(
        functools.partial(local, sizes),
        mesh=mesh,
        in_specs=(P("bz", "bxy", None), P(None, "bz", "bxy", None), P(), P(), P()),
        out_specs=P("bz", "bxy", None),
        check_vma=False,
    )
```

```python
import functools

import jax
import jax.numpy as jnp
from jax import lax
from jax.experimental import pallas as pl
from jax.experimental.pallas import tpu as pltpu

VIEWS = 3
RANK = 3
RADIUS = 4
TAPS = 9
PASSES = 8
ROUNDS = 3 + VIEWS
EPS_TV = 0.25
TAU = 0.08
BACKGROUND = 0.1
CZ, CX = 8, 16
ROWS = CZ * CX
FULL = (CZ + 2 * RADIUS) * (CX + 2 * RADIUS)
DIRS = [(-1, 0), (1, 0), (0, -1), (0, 1), (-1, -1), (-1, 1), (1, -1), (1, 1)]
BF = jnp.bfloat16
F32 = jnp.float32
SPOT = {
    (-1, 0): (128, 64),
    (1, 0): (192, 64),
    (0, -1): (256, 32),
    (0, 1): (288, 32),
    (-1, -1): (320, 16),
    (-1, 1): (336, 16),
    (1, -1): (352, 16),
    (1, 1): (368, 16),
}


def row_places():
    k = lax.broadcasted_iota(jnp.int32, (CZ + CX, FULL), 1)
    z, x = k // CX, k % CX
    for (dz, dx), (first, rows) in SPOT.items():
        q = k - first
        wide = CX if dx == 0 else RADIUS
        here = (q >= 0) & (q < rows)
        z = jnp.where(here, q // wide + (-RADIUS, 0, CZ)[dz + 1], z)
        x = jnp.where(here, q % wide + (-RADIUS, 0, CX)[dx + 1], x)
    row = lax.broadcasted_iota(jnp.int32, (CZ + CX, FULL), 0)
    return jnp.where(row < CZ, z - row, x - row + CZ) + RADIUS


def flux(diff):
    return diff * lax.rsqrt(diff * diff + EPS_TV)


def kernel(
    sizes, taps_in, shift_in, inter_in, est_in, obs_in, out,
    nat, u, pack, fields, strips, w_f, w_a, c_f, c_a, obs_r, tmp, img, corr,
    taps, shift, inter, est, obs, send_sems, recv_sems, in_sems,
):
    nz, nx = sizes
    iz, ix = lax.axis_index("bz"), lax.axis_index("bxy")
    ny = est.shape[2]
    loads = [
        pltpu.make_async_copy(a, b, in_sems.at[n])
        for n, (a, b) in enumerate(
            ((est_in, est), (taps_in, taps), (shift_in, shift), (inter_in, inter), (obs_in, obs)))
    ]
    for load in loads:
        load.start()

    def exists(d):
        dz, dx = d
        ok = None
        for step, at, count in ((dz, iz, nz), (dx, ix, nx)):
            if step:
                here = at > 0 if step < 0 else at < count - 1
                ok = here if ok is None else jnp.logical_and(ok, here)
        return ok

    def peer(d):
        return {"bz": iz + d[0], "bxy": ix + d[1]}

    def opposite(d):
        return (-d[0], -d[1])

    barrier = pltpu.get_barrier_semaphore()
    for d in DIRS:
        @pl.when(exists(d))
        def _():
            pl.semaphore_signal(barrier, inc=1, device_id=peer(d), device_id_type=pl.DeviceIdType.MESH)

    for d in DIRS:
        @pl.when(jnp.logical_not(exists(d)))
        def _():
            first, rows = SPOT[d]
            for k in range(ROUNDS):
                fields[k, first:first + rows] = jnp.zeros((rows, ny), BF)

    def fill(k, read):
        for z in range(CZ):
            fields[k, z * CX:(z + 1) * CX] = read(z).astype(BF)
            pack[0, 4 * z:4 * z + 4] = read(z)[0:4]
            pack[1, 4 * z:4 * z + 4] = read(z)[12:16]
        strips[k] = pack[...].astype(BF)

    loads[0].wait()
    fill(0, lambda z: est[z])

    wide_z = 3 - jnp.where(iz == 0, 1, 0) - jnp.where(iz == nz - 1, 1, 0)
    wide_x = 3 - jnp.where(ix == 0, 1, 0) - jnp.where(ix == nx - 1, 1, 0)
    pl.semaphore_wait(barrier, wide_z * wide_x - 1)

    def copy_of(k, n):
        d = DIRS[n]
        first, rows = SPOT[opposite(d)]
        if d[1] == 0:
            low = 0 if d[0] < 0 else 64
            src = fields.at[k, low:low + 64]
        else:
            side = 0 if d[1] < 0 else 1
            low = 0 if d[0] <= 0 else 16
            src = strips.at[k, side, low:low + rows]
        return pltpu.make_async_remote_copy(
            src_ref=src, dst_ref=fields.at[k, first:first + rows],
            send_sem=send_sems.at[k, n], recv_sem=recv_sems.at[k, n],
            device_id=peer(d), device_id_type=pl.DeviceIdType.MESH)

    def start(k):
        for n, d in enumerate(DIRS):
            @pl.when(exists(d))
            def _():
                copy_of(k, n).start()

    def finish_send(k):
        for n, d in enumerate(DIRS):
            @pl.when(exists(d))
            def _():
                copy_of(k, n).wait_send()

    def finish_recv(k):
        for n, d in enumerate(DIRS):
            @pl.when(exists(opposite(d)))
            def _():
                copy_of(k, n).wait_recv()

    start(0)

    lane = lax.broadcasted_iota(jnp.int32, (8, ny), 1)
    places = row_places()
    tap_z = places[0:CZ]
    tap_x = places[CZ:CZ + CX]

    def prepare(v):
        moved = (lane + shift[v]) & (ny - 1)
        for r in range(RANK):
            sums = []
            for axis in range(3):
                total = taps[v, r, axis, 0]
                for t in range(1, TAPS):
                    total = total + taps[v, r, axis, t]
                sums.append(total)
            for w, forward in ((w_f, True), (w_a, False)):
                a = jnp.zeros((CZ, FULL), F32)
                b = jnp.zeros((CX, FULL), F32)
                for t in range(TAPS):
                    at = t if forward else TAPS - 1 - t
                    a = jnp.where(tap_z == t, taps[v, r, 0, at], a)
                    b = jnp.where(tap_x == t, taps[v, r, 1, at], b)
                a = a / (sums[0] * RANK)
                b = b / sums[1]
                for zo in range(CZ):
                    whole = a[zo:zo + 1] * b
                    high = whole.astype(BF)
                    rows = pl.ds(r * ROWS + zo * CX, CX)
                    w[v, rows, 0:FULL] = high
                    w[v, rows, FULL:2 * FULL] = (whole - high.astype(F32)).astype(BF)
            scale = 1.0 / jnp.full((8, ny), sums[2], F32)
            for t in range(TAPS):
                value = scale * taps[v, r, 2, t]
                for c, place in ((c_f, moved - (t - RADIUS)), (c_a, moved + (t - RADIUS))):
                    inside = (place >= 0) & (place < ny)
                    c[v, r * TAPS + t] = jnp.where(inside, value, 0.0)
        back = (ny - shift[v]) & (ny - 1)
        for z in range(CZ):
            obs_r[v, z] = pltpu.roll(obs[v, z].astype(F32), back, 1)

    for load in loads[1:]:
        load.wait()
    prepare(0)
    finish_recv(0)

    columns = range(ny // 128)
    for c in columns:
        nat[4:12, c, 8:24] = est[:, :, 128 * c:128 * c + 128]

    def assemble(k):
        for c in columns:
            at = slice(128 * c, 128 * c + 128)
            for dz, dx in DIRS:
                first, rows = SPOT[(dz, dx)]
                piece = fields[k, first:first + rows, at].astype(F32)
                z0 = {-1: 0, 0: 4, 1: 12}[dz]
                if dx == 0:
                    nat[z0:z0 + 4, c, 8:24] = piece.reshape(4, 16, 128)
                else:
                    x0 = 4 if dx < 0 else 24
                    for z in range(rows // 4):
                        nat[z0 + z, c, x0:x0 + 4] = piece[4 * z:4 * z + 4]

        def relayout(z, carry):
            for i in range(3):
                for c in columns:
                    u[z, i, :, 128 * c:128 * c + 128] = nat[z, c, pl.ds(4 + i, 8, stride=3), :]
            return carry

        lax.fori_loop(0, 16, relayout, 0)

    sub = lax.broadcasted_iota(jnp.int32, (8, 128), 0)
    low_x = jnp.where(ix == 0, 0.0, 1.0)
    high_x = jnp.where(ix == nx - 1, 0.0, 1.0)
    masks = []
    for at, keep in ((1, low_x), (6, high_x)):
        masks.append(jnp.concatenate([jnp.where(sub == at, keep, 1.0)] * (ny // 128), axis=1))
    y_mask = jnp.where(lax.broadcasted_iota(jnp.int32, (8, 128), 1) == 127, 0.0, 1.0)

    def tv(p):
        @pl.when(iz == 0)
        def _():
            u[3] = u[4]

        @pl.when(iz == nz - 1)
        def _():
            u[12] = u[11]

        def planes(step, below):
            z0 = p + step * (8 - p)
            below = list(below)
            here = [u[z0, i] for i in range(3)]
            for z in range(8 - p):
                after = [u[z0 + z + 1, i] for i in range(3)]
                above = [flux(after[i] - here[i]) for i in range(3)]
                fx = [flux(here[i + 1] - here[i]) * masks[i] for i in range(2)]
                fx.append(flux(pltpu.roll(here[0], 7, 0) - here[2]))
                fx_low = [pltpu.roll(fx[2], 1, 0)] + fx[:2]
                for i in range(3):
                    fy = flux(pltpu.roll(here[i], ny - 1, 1) - here[i])
                    fy = jnp.concatenate([fy[:, :ny - 128], fy[:, ny - 128:] * y_mask], axis=1)
                    total = (above[i] - below[i]) + (fx[i] - fx_low[i]) + (fy - pltpu.roll(fy, 1, 1))
                    u[z0 + z, i] = here[i] + TAU * total
                here, below = after, above
            return tuple(below)

        first = tuple(flux(u[p, i] - u[p - 1, i]) for i in range(3))
        lax.fori_loop(0, 2, planes, first)

    def natural(z, carry):
        for i in range(3):
            for c in columns:
                nat[z, c, pl.ds(4 + i, 8, stride=3), :] = u[z, i, :, 128 * c:128 * c + 128]
        return carry

    for half in range(2):
        assemble(half)
        for p in range(1, PASSES // 2 + 1):
            tv(p)
        lax.fori_loop(4, 12, natural, 0)
        fill(half + 1, lambda z: jnp.concatenate([nat[4 + z, c, 8:24] for c in columns], axis=1))
        start(half + 1)
        prepare(half + 1)
        finish_recv(half + 1)

    f2d = jnp.concatenate([fields[2], fields[2]], axis=0)

    def along_y(c, v, j, sign):
        parts = [tmp[r, pl.ds(2 * j, 2)] for r in range(RANK)]
        total = None
        for t in range(TAPS):
            term = c[v, t] * parts[0]
            for r in range(1, RANK):
                term = term + c[v, r * TAPS + t] * parts[r]
            move = (sign * (t - RADIUS)) % ny
            if move:
                term = pltpu.roll(term, move, 2)
            total = term if total is None else total + term
        return total

    for v in range(VIEWS):
        tmp[...] = jnp.dot(w_f[v], f2d, preferred_element_type=F32).reshape(tmp.shape)
        flag = inter[v, ix, iz]

        def ratios(j, carry):
            image = along_y(c_f, v, j, -1)
            img[j] = jnp.where(flag > 0, obs_r[v, j] / (image.reshape(CX, ny) + BACKGROUND), 1.0)
            return carry

        lax.fori_loop(0, CZ, ratios, 0, unroll=2)
        fill(3 + v, lambda z: img[z])
        start(3 + v)

    for v in range(VIEWS):
        finish_recv(3 + v)
        f3d = jnp.concatenate([fields[3 + v], fields[3 + v]], axis=0)
        tmp[...] = jnp.dot(w_a[v], f3d, preferred_element_type=F32).reshape(tmp.shape)

        def spread(j, carry):
            back = along_y(c_a, v, j, 1).reshape(CX, ny)
            if v:
                back = back + corr[j]
            if v < VIEWS - 1:
                corr[j] = back
            else:
                smoothed = jnp.concatenate([nat[4 + j, c, 8:24] for c in columns], axis=1)
                out[j] = smoothed * back / VIEWS
            return carry

        lax.fori_loop(0, CZ, spread, 0, unroll=2)
    for k in range(ROUNDS):
        finish_send(k)


def local(sizes, estimate, observed, psf_taps, view_shift, intersection):
    cz, cx, ny = estimate.shape
    turned = intersection.transpose(0, 2, 1)
    vmem = pl.BlockSpec(memory_space=pltpu.VMEM)
    hbm = pl.BlockSpec(memory_space=pltpu.HBM)
    dma = pltpu.SemaphoreType.DMA
    return pl.pallas_call(
        functools.partial(kernel, sizes),
        out_shape=jax.ShapeDtypeStruct((cz, cx, ny), F32),
        in_specs=[hbm] * 5,
        out_specs=vmem,
        scratch_shapes=[
            pltpu.VMEM((16, ny // 128, 32, 128), F32),
            pltpu.VMEM((16, 3, 8, ny), F32),
            pltpu.VMEM((2, 32, ny), F32),
            pltpu.VMEM((ROUNDS, FULL, ny), BF),
            pltpu.VMEM((ROUNDS, 2, 32, ny), BF),
            pltpu.VMEM((VIEWS, RANK * ROWS, 2 * FULL), BF),
            pltpu.VMEM((VIEWS, RANK * ROWS, 2 * FULL), BF),
            pltpu.VMEM((VIEWS, RANK * TAPS, 8, ny), F32),
            pltpu.VMEM((VIEWS, RANK * TAPS, 8, ny), F32),
            pltpu.VMEM((VIEWS, cz, cx, ny), F32),
            pltpu.VMEM((RANK, 16, 8, ny), F32),
            pltpu.VMEM((CZ, CX, ny), F32),
            pltpu.VMEM((CZ, CX, ny), F32),
            pltpu.SMEM(psf_taps.shape, F32),
            pltpu.SMEM(view_shift.shape, jnp.int32),
            pltpu.SMEM(turned.shape, jnp.int32),
            pltpu.VMEM(estimate.shape, F32),
            pltpu.VMEM(observed.shape, BF),
            dma((ROUNDS, 8)), dma((ROUNDS, 8)), dma((5,)),
        ],
        compiler_params=pltpu.CompilerParams(
            collective_id=0, has_side_effects=True, vmem_limit_bytes=56 * 1024 * 1024),
        cost_estimate=pl.CostEstimate(flops=10**9, bytes_accessed=10**6, transcendentals=5 * 10**6),
    )(psf_taps, view_shift, turned, estimate, observed)


def solution(mesh):
    from jax.sharding import PartitionSpec as P
    sizes = (mesh.shape["bz"], mesh.shape["bxy"])
    return jax.shard_map(
        functools.partial(local, sizes),
        mesh=mesh,
        in_specs=(P("bz", "bxy", None), P(None, "bz", "bxy", None), P(), P(), P()),
        out_specs=P("bz", "bxy", None),
        check_vma=False,
    )
```

```python
import functools

import jax
import jax.numpy as jnp
from jax import lax
from jax.experimental import pallas as pl
from jax.experimental.pallas import tpu as pltpu

VIEWS = 3
RANK = 3
RADIUS = 4
TAPS = 9
PASSES = 8
ROUNDS = 3 + VIEWS
UNROLL = 8
EPS_TV = 0.25
TAU = 0.08
BACKGROUND = 0.1
CZ, CX = 8, 16
ROWS = CZ * CX
FULL = (CZ + 2 * RADIUS) * (CX + 2 * RADIUS)
DIRS = [(-1, 0), (1, 0), (0, -1), (0, 1), (-1, -1), (-1, 1), (1, -1), (1, 1)]
BF = jnp.bfloat16
F32 = jnp.float32
SPOT = {
    (-1, 0): (128, 64),
    (1, 0): (192, 64),
    (0, -1): (256, 32),
    (0, 1): (288, 32),
    (-1, -1): (320, 16),
    (-1, 1): (336, 16),
    (1, -1): (352, 16),
    (1, 1): (368, 16),
}


def row_places():
    k = lax.broadcasted_iota(jnp.int32, (CZ + CX, FULL), 1)
    z, x = k >> 4, k & (CX - 1)
    for (dz, dx), (first, rows) in SPOT.items():
        q = k - first
        bits = 4 if dx == 0 else 2
        here = (q >= 0) & (q < rows)
        z = jnp.where(here, (q >> bits) + (-RADIUS, 0, CZ)[dz + 1], z)
        x = jnp.where(here, (q & ((1 << bits) - 1)) + (-RADIUS, 0, CX)[dx + 1], x)
    row = lax.broadcasted_iota(jnp.int32, (CZ + CX, FULL), 0)
    return jnp.where(row < CZ, z - row, x - row + CZ) + RADIUS


def flux(diff):
    return diff * lax.rsqrt(diff * diff + EPS_TV)


def kernel(
    sizes, taps_in, shift_in, inter_in, est_in, obs_in, out,
    nat, u, pack, fields, strips, w_f, w_a, c_f, c_a, obs_r, tmp, img, corr,
    taps, shift, inter, est, obs, send_sems, recv_sems, in_sems,
):
    nz, nx = sizes
    iz, ix = lax.axis_index("bz"), lax.axis_index("bxy")
    ny = est.shape[2]
    loads = [
        pltpu.make_async_copy(a, b, in_sems.at[n])
        for n, (a, b) in enumerate(
            ((est_in, est), (taps_in, taps), (shift_in, shift), (inter_in, inter), (obs_in, obs)))
    ]
    for load in loads:
        load.start()

    def exists(d):
        dz, dx = d
        ok = None
        for step, at, count in ((dz, iz, nz), (dx, ix, nx)):
            if step:
                here = at > 0 if step < 0 else at < count - 1
                ok = here if ok is None else jnp.logical_and(ok, here)
        return ok

    def peer(d):
        return {"bz": iz + d[0], "bxy": ix + d[1]}

    def opposite(d):
        return (-d[0], -d[1])

    barrier = pltpu.get_barrier_semaphore()
    for d in DIRS:
        @pl.when(exists(d))
        def _():
            pl.semaphore_signal(barrier, inc=1, device_id=peer(d), device_id_type=pl.DeviceIdType.MESH)

    for d in DIRS:
        @pl.when(jnp.logical_not(exists(d)))
        def _():
            first, rows = SPOT[d]
            for k in range(ROUNDS):
                fields[k, first:first + rows] = jnp.zeros((rows, ny), BF)

    def fill(k, read):
        for z in range(CZ):
            fields[k, z * CX:(z + 1) * CX] = read(z).astype(BF)
            pack[0, 4 * z:4 * z + 4] = read(z)[0:4]
            pack[1, 4 * z:4 * z + 4] = read(z)[12:16]
        strips[k] = pack[...].astype(BF)

    loads[0].wait()
    fill(0, lambda z: est[z])

    wide_z = 3 - jnp.where(iz == 0, 1, 0) - jnp.where(iz == nz - 1, 1, 0)
    wide_x = 3 - jnp.where(ix == 0, 1, 0) - jnp.where(ix == nx - 1, 1, 0)
    pl.semaphore_wait(barrier, wide_z * wide_x - 1)

    def copy_of(k, n):
        d = DIRS[n]
        first, rows = SPOT[opposite(d)]
        if d[1] == 0:
            low = 0 if d[0] < 0 else 64
            src = fields.at[k, low:low + 64]
        else:
            side = 0 if d[1] < 0 else 1
            low = 0 if d[0] <= 0 else 16
            src = strips.at[k, side, low:low + rows]
        return pltpu.make_async_remote_copy(
            src_ref=src, dst_ref=fields.at[k, first:first + rows],
            send_sem=send_sems.at[k, n], recv_sem=recv_sems.at[k, n],
            device_id=peer(d), device_id_type=pl.DeviceIdType.MESH)

    def start(k):
        for n, d in enumerate(DIRS):
            @pl.when(exists(d))
            def _():
                copy_of(k, n).start()

    def finish_send(k):
        for n, d in enumerate(DIRS):
            @pl.when(exists(d))
            def _():
                copy_of(k, n).wait_send()

    def finish_recv(k):
        for n, d in enumerate(DIRS):
            @pl.when(exists(opposite(d)))
            def _():
                copy_of(k, n).wait_recv()

    start(0)

    lane = lax.broadcasted_iota(jnp.int32, (8, ny), 1)
    places = row_places()
    tap_z = places[0:CZ]
    tap_x = places[CZ:CZ + CX]

    def prepare(v):
        moved = (lane + shift[v]) & (ny - 1)
        for r in range(RANK):
            sums = []
            for axis in range(3):
                total = taps[v, r, axis, 0]
                for t in range(1, TAPS):
                    total = total + taps[v, r, axis, t]
                sums.append(total)
            for w, forward in ((w_f, True), (w_a, False)):
                a = jnp.zeros((CZ, FULL), F32)
                b = jnp.zeros((CX, FULL), F32)
                for t in range(TAPS):
                    at = t if forward else TAPS - 1 - t
                    a = jnp.where(tap_z == t, taps[v, r, 0, at], a)
                    b = jnp.where(tap_x == t, taps[v, r, 1, at], b)
                a = a / (sums[0] * RANK)
                b = b / sums[1]
                for zo in range(CZ):
                    whole = a[zo:zo + 1] * b
                    high = whole.astype(BF)
                    rows = pl.ds(r * ROWS + zo * CX, CX)
                    w[v, rows, 0:FULL] = high
                    w[v, rows, FULL:2 * FULL] = (whole - high.astype(F32)).astype(BF)
            scale = 1.0 / jnp.full((8, ny), sums[2], F32)
            for t in range(TAPS):
                value = scale * taps[v, r, 2, t]
                for c, place in ((c_f, moved - (t - RADIUS)), (c_a, moved + (t - RADIUS))):
                    inside = (place >= 0) & (place < ny)
                    c[v, r * TAPS + t] = jnp.where(inside, value, 0.0)
        back = (ny - shift[v]) & (ny - 1)
        for z in range(CZ):
            obs_r[v, z] = pltpu.roll(obs[v, z].astype(F32), back, 1)

    for load in loads[1:]:
        load.wait()
    prepare(0)
    finish_recv(0)

    columns = range(ny // 128)
    for c in columns:
        nat[4:12, c, 8:24] = est[:, :, 128 * c:128 * c + 128]

    def assemble(k):
        for c in columns:
            at = slice(128 * c, 128 * c + 128)
            for dz, dx in DIRS:
                first, rows = SPOT[(dz, dx)]
                piece = fields[k, first:first + rows, at].astype(F32)
                z0 = {-1: 0, 0: 4, 1: 12}[dz]
                if dx == 0:
                    nat[z0:z0 + 4, c, 8:24] = piece.reshape(4, 16, 128)
                else:
                    x0 = 4 if dx < 0 else 24
                    for z in range(rows // 4):
                        nat[z0 + z, c, x0:x0 + 4] = piece[4 * z:4 * z + 4]

        def relayout(z, carry):
            for i in range(3):
                for c in columns:
                    u[z, i, :, 128 * c:128 * c + 128] = nat[z, c, pl.ds(4 + i, 8, stride=3), :]
            return carry

        lax.fori_loop(0, 16, relayout, 0)

    sub = lax.broadcasted_iota(jnp.int32, (8, 128), 0)
    low_x = jnp.where(ix == 0, 0.0, 1.0)
    high_x = jnp.where(ix == nx - 1, 0.0, 1.0)
    masks = []
    for at, keep in ((1, low_x), (6, high_x)):
        masks.append(jnp.concatenate([jnp.where(sub == at, keep, 1.0)] * (ny // 128), axis=1))
    y_mask = jnp.where(lax.broadcasted_iota(jnp.int32, (8, 128), 1) == 127, 0.0, 1.0)

    def tv(p):
        @pl.when(iz == 0)
        def _():
            u[3] = u[4]

        @pl.when(iz == nz - 1)
        def _():
            u[12] = u[11]

        def planes(below):
            z0 = p
            below = list(below)
            here = [u[z0, i] for i in range(3)]
            for z in range(16 - 2 * p):
                after = [u[z0 + z + 1, i] for i in range(3)]
                above = [flux(after[i] - here[i]) for i in range(3)]
                fx = [flux(here[i + 1] - here[i]) * masks[i] for i in range(2)]
                fx.append(flux(pltpu.roll(here[0], 7, 0) - here[2]))
                fx_low = [pltpu.roll(fx[2], 1, 0)] + fx[:2]
                for i in range(3):
                    fy = flux(pltpu.roll(here[i], ny - 1, 1) - here[i])
                    fy = jnp.concatenate([fy[:, :ny - 128], fy[:, ny - 128:] * y_mask], axis=1)
                    total = (above[i] - below[i]) + (fx[i] - fx_low[i]) + (fy - pltpu.roll(fy, 1, 1))
                    u[z0 + z, i] = here[i] + TAU * total
                here, below = after, above

        first = tuple(flux(u[p, i] - u[p - 1, i]) for i in range(3))
        planes(first)

    def natural(z, carry):
        for i in range(3):
            for c in columns:
                nat[z, c, pl.ds(4 + i, 8, stride=3), :] = u[z, i, :, 128 * c:128 * c + 128]
        return carry

    for half in range(2):
        assemble(half)
        for p in range(1, PASSES // 2 + 1):
            tv(p)
        lax.fori_loop(4, 12, natural, 0)
        fill(half + 1, lambda z: jnp.concatenate([nat[4 + z, c, 8:24] for c in columns], axis=1))
        start(half + 1)
        prepare(half + 1)
        finish_recv(half + 1)

    f2d = jnp.concatenate([fields[2], fields[2]], axis=0)

    def along_y(c, v, j, sign):
        parts = [tmp[v % 2, r, pl.ds(2 * j, 2)] for r in range(RANK)]
        total = None
        for t in range(TAPS):
            term = c[v, t] * parts[0]
            for r in range(1, RANK):
                term = term + c[v, r * TAPS + t] * parts[r]
            move = (sign * (t - RADIUS)) % ny
            if move:
                term = pltpu.roll(term, move, 2)
            total = term if total is None else total + term
        return total

    def mix_planes(w, v, field):
        tmp[v % 2] = jnp.dot(w[v], field, preferred_element_type=F32).reshape(tmp.shape[1:])

    mix_planes(w_f, 0, f2d)
    for v in range(VIEWS):
        if v + 1 < VIEWS:
            mix_planes(w_f, v + 1, f2d)
        flag = inter[v, ix, iz]

        def ratios(j, carry):
            image = along_y(c_f, v, j, -1)
            img[j] = jnp.where(flag > 0, obs_r[v, j] / (image.reshape(CX, ny) + BACKGROUND), 1.0)
            return carry

        lax.fori_loop(0, CZ, ratios, 0, unroll=UNROLL)
        fill(3 + v, lambda z: img[z])
        start(3 + v)

    for v in range(VIEWS):
        for w in ((0, 1), (), (2,))[v]:
            finish_recv(3 + w)
            mix_planes(w_a, w, jnp.concatenate([fields[3 + w], fields[3 + w]], axis=0))

        def spread(j, carry):
            back = along_y(c_a, v, j, 1).reshape(CX, ny)
            if v:
                back = back + corr[j]
            if v < VIEWS - 1:
                corr[j] = back
            else:
                smoothed = jnp.concatenate([nat[4 + j, c, 8:24] for c in columns], axis=1)
                out[j] = smoothed * back / VIEWS
            return carry

        lax.fori_loop(0, CZ, spread, 0, unroll=UNROLL)
    for k in range(ROUNDS):
        finish_send(k)


def local(sizes, estimate, observed, psf_taps, view_shift, intersection):
    cz, cx, ny = estimate.shape
    turned = intersection.transpose(0, 2, 1)
    vmem = pl.BlockSpec(memory_space=pltpu.VMEM)
    hbm = pl.BlockSpec(memory_space=pltpu.HBM)
    dma = pltpu.SemaphoreType.DMA
    return pl.pallas_call(
        functools.partial(kernel, sizes),
        out_shape=jax.ShapeDtypeStruct((cz, cx, ny), F32),
        in_specs=[hbm] * 5,
        out_specs=vmem,
        scratch_shapes=[
            pltpu.VMEM((16, ny // 128, 32, 128), F32),
            pltpu.VMEM((16, 3, 8, ny), F32),
            pltpu.VMEM((2, 32, ny), F32),
            pltpu.VMEM((ROUNDS, FULL, ny), BF),
            pltpu.VMEM((ROUNDS, 2, 32, ny), BF),
            pltpu.VMEM((VIEWS, RANK * ROWS, 2 * FULL), BF),
            pltpu.VMEM((VIEWS, RANK * ROWS, 2 * FULL), BF),
            pltpu.VMEM((VIEWS, RANK * TAPS, 8, ny), F32),
            pltpu.VMEM((VIEWS, RANK * TAPS, 8, ny), F32),
            pltpu.VMEM((VIEWS, cz, cx, ny), F32),
            pltpu.VMEM((2, RANK, 16, 8, ny), F32),
            pltpu.VMEM((CZ, CX, ny), F32),
            pltpu.VMEM((CZ, CX, ny), F32),
            pltpu.SMEM(psf_taps.shape, F32),
            pltpu.SMEM(view_shift.shape, jnp.int32),
            pltpu.SMEM(turned.shape, jnp.int32),
            pltpu.VMEM(estimate.shape, F32),
            pltpu.VMEM(observed.shape, BF),
            dma((ROUNDS, 8)), dma((ROUNDS, 8)), dma((5,)),
        ],
        compiler_params=pltpu.CompilerParams(
            collective_id=0, has_side_effects=True, vmem_limit_bytes=56 * 1024 * 1024),
        cost_estimate=pl.CostEstimate(flops=10**9, bytes_accessed=10**6, transcendentals=5 * 10**6),
    )(psf_taps, view_shift, turned, estimate, observed)


def solution(mesh):
    from jax.sharding import PartitionSpec as P
    sizes = (mesh.shape["bz"], mesh.shape["bxy"])
    return jax.shard_map(
        functools.partial(local, sizes),
        mesh=mesh,
        in_specs=(P("bz", "bxy", None), P(None, "bz", "bxy", None), P(), P(), P()),
        out_specs=P("bz", "bxy", None),
        check_vma=False,
    )
```

```python
import functools

import jax
import jax.numpy as jnp
from jax import lax
from jax.experimental import pallas as pl
from jax.experimental.pallas import tpu as pltpu

VIEWS = 3
RANK = 3
RADIUS = 4
TAPS = 9
PASSES = 8
ROUNDS = 3 + VIEWS
EPS_TV = 0.25
TAU = 0.08
BACKGROUND = 0.1
CZ, CX = 8, 16
ROWS = CZ * CX
FULL = (CZ + 2 * RADIUS) * (CX + 2 * RADIUS)
DIRS = [(-1, 0), (1, 0), (0, -1), (0, 1), (-1, -1), (-1, 1), (1, -1), (1, 1)]
BF = jnp.bfloat16
F32 = jnp.float32
SPOT = {
    (-1, 0): (128, 64),
    (1, 0): (192, 64),
    (0, -1): (256, 32),
    (0, 1): (288, 32),
    (-1, -1): (320, 16),
    (-1, 1): (336, 16),
    (1, -1): (352, 16),
    (1, 1): (368, 16),
}


def row_places():
    k = lax.broadcasted_iota(jnp.int32, (CZ + CX, FULL), 1)
    z, x = k >> 4, k & (CX - 1)
    for (dz, dx), (first, rows) in SPOT.items():
        q = k - first
        bits = 4 if dx == 0 else 2
        here = (q >= 0) & (q < rows)
        z = jnp.where(here, (q >> bits) + (-RADIUS, 0, CZ)[dz + 1], z)
        x = jnp.where(here, (q & ((1 << bits) - 1)) + (-RADIUS, 0, CX)[dx + 1], x)
    row = lax.broadcasted_iota(jnp.int32, (CZ + CX, FULL), 0)
    return jnp.where(row < CZ, z - row, x - row + CZ) + RADIUS


def flux(diff):
    return diff * lax.rsqrt(diff * diff + EPS_TV)


def kernel(
    sizes, taps_in, shift_in, inter_in, est_in, obs_in, out,
    nat, u, pack, fields, strips, w_f, w_a, c_f, c_a, obs_r, tmp, img, corr,
    taps, shift, inter, est, obs, send_sems, recv_sems, in_sems,
):
    nz, nx = sizes
    iz, ix = lax.axis_index("bz"), lax.axis_index("bxy")
    ny = est.shape[2]
    loads = [
        pltpu.make_async_copy(a, b, in_sems.at[n])
        for n, (a, b) in enumerate(
            ((est_in, est), (taps_in, taps), (shift_in, shift), (inter_in, inter), (obs_in, obs)))
    ]
    for load in loads:
        load.start()

    def exists(d):
        dz, dx = d
        ok = None
        for step, at, count in ((dz, iz, nz), (dx, ix, nx)):
            if step:
                here = at > 0 if step < 0 else at < count - 1
                ok = here if ok is None else jnp.logical_and(ok, here)
        return ok

    def peer(d):
        return {"bz": iz + d[0], "bxy": ix + d[1]}

    def opposite(d):
        return (-d[0], -d[1])

    barrier = pltpu.get_barrier_semaphore()
    for d in DIRS:
        @pl.when(exists(d))
        def _():
            pl.semaphore_signal(barrier, inc=1, device_id=peer(d), device_id_type=pl.DeviceIdType.MESH)

    for d in DIRS:
        @pl.when(jnp.logical_not(exists(d)))
        def _():
            first, rows = SPOT[d]
            for k in range(ROUNDS):
                fields[k, first:first + rows] = jnp.zeros((rows, ny), BF)

    def fill(k, read):
        for z in range(CZ):
            fields[k, z * CX:(z + 1) * CX] = read(z).astype(BF)
            pack[0, 4 * z:4 * z + 4] = read(z)[0:4]
            pack[1, 4 * z:4 * z + 4] = read(z)[12:16]
        strips[k] = pack[...].astype(BF)

    loads[0].wait()
    fill(0, lambda z: est[z])

    wide_z = 3 - jnp.where(iz == 0, 1, 0) - jnp.where(iz == nz - 1, 1, 0)
    wide_x = 3 - jnp.where(ix == 0, 1, 0) - jnp.where(ix == nx - 1, 1, 0)
    pl.semaphore_wait(barrier, wide_z * wide_x - 1)

    def copy_of(k, n):
        d = DIRS[n]
        first, rows = SPOT[opposite(d)]
        if d[1] == 0:
            low = 0 if d[0] < 0 else 64
            src = fields.at[k, low:low + 64]
        else:
            side = 0 if d[1] < 0 else 1
            low = 0 if d[0] <= 0 else 16
            src = strips.at[k, side, low:low + rows]
        return pltpu.make_async_remote_copy(
            src_ref=src, dst_ref=fields.at[k, first:first + rows],
            send_sem=send_sems.at[k, n], recv_sem=recv_sems.at[k, n],
            device_id=peer(d), device_id_type=pl.DeviceIdType.MESH)

    def start(k):
        for n, d in enumerate(DIRS):
            @pl.when(exists(d))
            def _():
                copy_of(k, n).start()

    def finish_send(k):
        for n, d in enumerate(DIRS):
            @pl.when(exists(d))
            def _():
                copy_of(k, n).wait_send()

    def finish_recv(k):
        for n, d in enumerate(DIRS):
            @pl.when(exists(opposite(d)))
            def _():
                copy_of(k, n).wait_recv()


    lane = lax.broadcasted_iota(jnp.int32, (8, ny), 1)
    places = row_places()
    tap_z = places[0:CZ]
    tap_x = places[CZ:CZ + CX]

    def prepare(v):
        moved = (lane + shift[v]) & (ny - 1)
        for r in range(RANK):
            sums = []
            for axis in range(3):
                total = taps[v, r, axis, 0]
                for t in range(1, TAPS):
                    total = total + taps[v, r, axis, t]
                sums.append(total)
            for w, forward in ((w_f, True), (w_a, False)):
                a = jnp.zeros((CZ, FULL), F32)
                b = jnp.zeros((CX, FULL), F32)
                for t in range(TAPS):
                    at = t if forward else TAPS - 1 - t
                    a = jnp.where(tap_z == t, taps[v, r, 0, at], a)
                    b = jnp.where(tap_x == t, taps[v, r, 1, at], b)
                a = a / (sums[0] * RANK)
                b = b / sums[1]
                for zo in range(CZ):
                    whole = a[zo:zo + 1] * b
                    high = whole.astype(BF)
                    rows = pl.ds(r * ROWS + zo * CX, CX)
                    w[v, rows, 0:FULL] = high
                    w[v, rows, FULL:2 * FULL] = (whole - high.astype(F32)).astype(BF)
            scale = 1.0 / jnp.full((8, ny), sums[2], F32)
            for t in range(TAPS):
                value = scale * taps[v, r, 2, t]
                for c, place in ((c_f, moved - (t - RADIUS)), (c_a, moved + (t - RADIUS))):
                    inside = (place >= 0) & (place < ny)
                    c[v, r * TAPS + t] = jnp.where(inside, value, 0.0)
        back = (ny - shift[v]) & (ny - 1)
        for z in range(CZ):
            obs_r[v, z] = pltpu.roll(obs[v, z].astype(F32), back, 1)

    columns = range(ny // 128)
    for c in columns:
        nat[4:12, c, 8:24] = est[:, :, 128 * c:128 * c + 128]

    def assemble(k):
        for c in columns:
            at = slice(128 * c, 128 * c + 128)
            for dz, dx in DIRS:
                first, rows = SPOT[(dz, dx)]
                piece = fields[k, first:first + rows, at].astype(F32)
                z0 = {-1: 0, 0: 4, 1: 12}[dz]
                if dx == 0:
                    nat[z0:z0 + 4, c, 8:24] = piece.reshape(4, 16, 128)
                else:
                    x0 = 4 if dx < 0 else 24
                    for z in range(rows // 4):
                        nat[z0 + z, c, x0:x0 + 4] = piece[4 * z:4 * z + 4]

        def relayout(z, carry):
            for i in range(3):
                for c in columns:
                    u[z, i, :, 128 * c:128 * c + 128] = nat[z, c, pl.ds(4 + i, 8, stride=3), :]
            return carry

        lax.fori_loop(0, 16, relayout, 0)

    sub = lax.broadcasted_iota(jnp.int32, (8, 128), 0)
    low_x = jnp.where(ix == 0, 0.0, 1.0)
    high_x = jnp.where(ix == nx - 1, 0.0, 1.0)
    masks = []
    for at, keep in ((1, low_x), (6, high_x)):
        masks.append(jnp.concatenate([jnp.where(sub == at, keep, 1.0)] * (ny // 128), axis=1))
    y_mask = jnp.where(lax.broadcasted_iota(jnp.int32, (8, 128), 1) == 127, 0.0, 1.0)

    def tv(p):
        @pl.when(iz == 0)
        def _():
            u[3] = u[4]

        @pl.when(iz == nz - 1)
        def _():
            u[12] = u[11]

        def planes(step, below):
            z0 = p + step * (8 - p)
            below = list(below)
            here = [u[z0, i] for i in range(3)]
            for z in range(8 - p):
                after = [u[z0 + z + 1, i] for i in range(3)]
                above = [flux(after[i] - here[i]) for i in range(3)]
                fx = [flux(here[i + 1] - here[i]) * masks[i] for i in range(2)]
                fx.append(flux(pltpu.roll(here[0], 7, 0) - here[2]))
                fx_low = [pltpu.roll(fx[2], 1, 0)] + fx[:2]
                for i in range(3):
                    fy = flux(pltpu.roll(here[i], ny - 1, 1) - here[i])
                    fy = jnp.concatenate([fy[:, :ny - 128], fy[:, ny - 128:] * y_mask], axis=1)
                    total = (above[i] - below[i]) + (fx[i] - fx_low[i]) + (fy - pltpu.roll(fy, 1, 1))
                    u[z0 + z, i] = here[i] + TAU * total
                here, below = after, above
            return tuple(below)

        first = tuple(flux(u[p, i] - u[p - 1, i]) for i in range(3))
        lax.fori_loop(0, 2, planes, first)

    def natural(z, carry):
        for i in range(3):
            for c in columns:
                nat[z, c, pl.ds(4 + i, 8, stride=3), :] = u[z, i, :, 128 * c:128 * c + 128]
        return carry

    def rim(k, carry):
        start(k)

        @pl.when(k == 0)
        def _():
            for load in loads[1:]:
                load.wait()

        prepare(k)
        finish_recv(k)

        @pl.when(k < 2)
        def _():
            assemble(k)
            for p in range(1, PASSES // 2 + 1):
                tv(p)
            lax.fori_loop(4, 12, natural, 0)
            fill(k + 1, lambda z: jnp.concatenate([nat[4 + z, c, 8:24] for c in columns], axis=1))

        return carry

    lax.fori_loop(0, 3, rim, 0)

    def f2d(k):
        field = fields[k]
        return jnp.concatenate([field, field], axis=0)

    def along_y(c, v, j, sign):
        parts = [tmp[r, pl.ds(2 * j, 2)] for r in range(RANK)]
        total = None
        for t in range(TAPS):
            term = c[v, t] * parts[0]
            for r in range(1, RANK):
                term = term + c[v, r * TAPS + t] * parts[r]
            move = (sign * (t - RADIUS)) % ny
            if move:
                term = pltpu.roll(term, move, 2)
            total = term if total is None else total + term
        return total

    def forward(v, carry):
        tmp[...] = jnp.dot(w_f[v], f2d(2), preferred_element_type=F32).reshape(tmp.shape)
        flag = inter[v, ix, iz]

        def ratios(j, carry):
            image = along_y(c_f, v, j, -1)
            img[j] = jnp.where(flag > 0, obs_r[v, j] / (image.reshape(CX, ny) + BACKGROUND), 1.0)
            return carry

        lax.fori_loop(0, CZ, ratios, 0, unroll=2)
        fill(3 + v, lambda z: img[z])
        start(3 + v)
        return carry

    lax.fori_loop(0, VIEWS, forward, 0)
    corr[...] = jnp.zeros(corr.shape, F32)

    def adjoint(v, carry):
        finish_recv(3 + v)
        tmp[...] = jnp.dot(w_a[v], f2d(3 + v), preferred_element_type=F32).reshape(tmp.shape)

        def spread(j, carry):
            corr[j] = corr[j] + along_y(c_a, v, j, 1).reshape(CX, ny)
            return carry

        lax.fori_loop(0, CZ, spread, 0, unroll=2)
        return carry

    lax.fori_loop(0, VIEWS, adjoint, 0)

    def finish(z, carry):
        smoothed = jnp.concatenate([nat[4 + z, c, 8:24] for c in columns], axis=1)
        out[z] = smoothed * corr[z] / VIEWS
        return carry

    lax.fori_loop(0, CZ, finish, 0)

    def sent_all(k, carry):
        finish_send(k)
        return carry

    lax.fori_loop(0, ROUNDS, sent_all, 0)


def local(sizes, estimate, observed, psf_taps, view_shift, intersection):
    cz, cx, ny = estimate.shape
    turned = intersection.transpose(0, 2, 1)
    vmem = pl.BlockSpec(memory_space=pltpu.VMEM)
    hbm = pl.BlockSpec(memory_space=pltpu.HBM)
    dma = pltpu.SemaphoreType.DMA
    return pl.pallas_call(
        functools.partial(kernel, sizes),
        out_shape=jax.ShapeDtypeStruct((cz, cx, ny), F32),
        in_specs=[hbm] * 5,
        out_specs=vmem,
        scratch_shapes=[
            pltpu.VMEM((16, ny // 128, 32, 128), F32),
            pltpu.VMEM((16, 3, 8, ny), F32),
            pltpu.VMEM((2, 32, ny), F32),
            pltpu.VMEM((ROUNDS, FULL, ny), BF),
            pltpu.VMEM((ROUNDS, 2, 32, ny), BF),
            pltpu.VMEM((VIEWS, RANK * ROWS, 2 * FULL), BF),
            pltpu.VMEM((VIEWS, RANK * ROWS, 2 * FULL), BF),
            pltpu.VMEM((VIEWS, RANK * TAPS, 8, ny), F32),
            pltpu.VMEM((VIEWS, RANK * TAPS, 8, ny), F32),
            pltpu.VMEM((VIEWS, cz, cx, ny), F32),
            pltpu.VMEM((RANK, 16, 8, ny), F32),
            pltpu.VMEM((CZ, CX, ny), F32),
            pltpu.VMEM((CZ, CX, ny), F32),
            pltpu.SMEM(psf_taps.shape, F32),
            pltpu.SMEM(view_shift.shape, jnp.int32),
            pltpu.SMEM(turned.shape, jnp.int32),
            pltpu.VMEM(estimate.shape, F32),
            pltpu.VMEM(observed.shape, BF),
            dma((ROUNDS, 8)), dma((ROUNDS, 8)), dma((5,)),
        ],
        compiler_params=pltpu.CompilerParams(
            collective_id=0, has_side_effects=True, vmem_limit_bytes=56 * 1024 * 1024),
        cost_estimate=pl.CostEstimate(flops=10**9, bytes_accessed=10**6, transcendentals=5 * 10**6),
    )(psf_taps, view_shift, turned, estimate, observed)


def solution(mesh):
    from jax.sharding import PartitionSpec as P
    sizes = (mesh.shape["bz"], mesh.shape["bxy"])
    return jax.shard_map(
        functools.partial(local, sizes),
        mesh=mesh,
        in_specs=(P("bz", "bxy", None), P(None, "bz", "bxy", None), P(), P(), P()),
        out_specs=P("bz", "bxy", None),
        check_vma=False,
    )
```

```python
import functools

import jax
import jax.numpy as jnp
from jax import lax
from jax.experimental import pallas as pl
from jax.experimental.pallas import tpu as pltpu

VIEWS = 3
RANK = 3
RADIUS = 4
TAPS = 9
PASSES = 8
ROUNDS = 3 + VIEWS
EPS_TV = 0.25
TAU = 0.08
BACKGROUND = 0.1
CZ, CX = 8, 16
ROWS = CZ * CX
FULL = (CZ + 2 * RADIUS) * (CX + 2 * RADIUS)
DIRS = [(-1, 0), (1, 0), (0, -1), (0, 1), (-1, -1), (-1, 1), (1, -1), (1, 1)]
BF = jnp.bfloat16
F32 = jnp.float32
SPOT = {
    (-1, 0): (128, 64),
    (1, 0): (192, 64),
    (0, -1): (256, 32),
    (0, 1): (288, 32),
    (-1, -1): (320, 16),
    (-1, 1): (336, 16),
    (1, -1): (352, 16),
    (1, 1): (368, 16),
}


def row_places():
    k = lax.broadcasted_iota(jnp.int32, (CZ + CX, FULL), 1)
    z, x = k >> 4, k & (CX - 1)
    for (dz, dx), (first, rows) in SPOT.items():
        q = k - first
        bits = 4 if dx == 0 else 2
        here = (q >= 0) & (q < rows)
        z = jnp.where(here, (q >> bits) + (-RADIUS, 0, CZ)[dz + 1], z)
        x = jnp.where(here, (q & ((1 << bits) - 1)) + (-RADIUS, 0, CX)[dx + 1], x)
    row = lax.broadcasted_iota(jnp.int32, (CZ + CX, FULL), 0)
    return jnp.where(row < CZ, z - row, x - row + CZ) + RADIUS


def flux(diff):
    return diff * lax.rsqrt(diff * diff + EPS_TV)


def kernel(
    sizes, taps_in, shift_in, inter_in, est_in, obs_in, out,
    nat, u, pack, fields, strips, w_f, w_a, c_f, c_a, obs_r, tmp, img, corr,
    taps, shift, inter, est, obs, send_sems, recv_sems, in_sems,
):
    nz, nx = sizes
    iz, ix = lax.axis_index("bz"), lax.axis_index("bxy")
    ny = est.shape[2]
    loads = [
        pltpu.make_async_copy(a, b, in_sems.at[n])
        for n, (a, b) in enumerate(
            ((est_in, est), (taps_in, taps), (shift_in, shift), (inter_in, inter), (obs_in, obs)))
    ]
    for load in loads:
        load.start()

    def exists(d):
        dz, dx = d
        ok = None
        for step, at, count in ((dz, iz, nz), (dx, ix, nx)):
            if step:
                here = at > 0 if step < 0 else at < count - 1
                ok = here if ok is None else jnp.logical_and(ok, here)
        return ok

    def peer(d):
        return {"bz": iz + d[0], "bxy": ix + d[1]}

    def opposite(d):
        return (-d[0], -d[1])

    barrier = pltpu.get_barrier_semaphore()
    for d in DIRS:
        @pl.when(exists(d))
        def _():
            pl.semaphore_signal(barrier, inc=1, device_id=peer(d), device_id_type=pl.DeviceIdType.MESH)

    for d in DIRS:
        @pl.when(jnp.logical_not(exists(d)))
        def _():
            first, rows = SPOT[d]
            for k in range(ROUNDS):
                fields[k, first:first + rows] = jnp.zeros((rows, ny), BF)

    def fill(k, read):
        for z in range(CZ):
            fields[k, z * CX:(z + 1) * CX] = read(z).astype(BF)
            pack[0, 4 * z:4 * z + 4] = read(z)[0:4]
            pack[1, 4 * z:4 * z + 4] = read(z)[12:16]
        strips[k] = pack[...].astype(BF)

    loads[0].wait()
    fill(0, lambda z: est[z])

    wide_z = 3 - jnp.where(iz == 0, 1, 0) - jnp.where(iz == nz - 1, 1, 0)
    wide_x = 3 - jnp.where(ix == 0, 1, 0) - jnp.where(ix == nx - 1, 1, 0)
    pl.semaphore_wait(barrier, wide_z * wide_x - 1)

    def copy_of(k, n):
        d = DIRS[n]
        first, rows = SPOT[opposite(d)]
        if d[1] == 0:
            low = 0 if d[0] < 0 else 64
            src = fields.at[k, low:low + 64]
        else:
            side = 0 if d[1] < 0 else 1
            low = 0 if d[0] <= 0 else 16
            src = strips.at[k, side, low:low + rows]
        return pltpu.make_async_remote_copy(
            src_ref=src, dst_ref=fields.at[k, first:first + rows],
            send_sem=send_sems.at[k, n], recv_sem=recv_sems.at[k, n],
            device_id=peer(d), device_id_type=pl.DeviceIdType.MESH)

    def start(k):
        for n, d in enumerate(DIRS):
            @pl.when(exists(d))
            def _():
                copy_of(k, n).start()

    def finish_send(k):
        for n, d in enumerate(DIRS):
            @pl.when(exists(d))
            def _():
                copy_of(k, n).wait_send()

    def finish_recv(k):
        for n, d in enumerate(DIRS):
            @pl.when(exists(opposite(d)))
            def _():
                copy_of(k, n).wait_recv()


    lane = lax.broadcasted_iota(jnp.int32, (8, ny), 1)
    places = row_places()
    tap_z = places[0:CZ]
    tap_x = places[CZ:CZ + CX]

    def prepare(v):
        moved = (lane + shift[v]) & (ny - 1)
        for r in range(RANK):
            sums = []
            for axis in range(3):
                total = taps[v, r, axis, 0]
                for t in range(1, TAPS):
                    total = total + taps[v, r, axis, t]
                sums.append(total)
            for w, forward in ((w_f, True), (w_a, False)):
                a = jnp.zeros((CZ, FULL), F32)
                b = jnp.zeros((CX, FULL), F32)
                for t in range(TAPS):
                    at = t if forward else TAPS - 1 - t
                    a = jnp.where(tap_z == t, taps[v, r, 0, at], a)
                    b = jnp.where(tap_x == t, taps[v, r, 1, at], b)
                a = a / (sums[0] * RANK)
                b = b / sums[1]
                for zo in range(CZ):
                    whole = a[zo:zo + 1] * b
                    high = whole.astype(BF)
                    rows = pl.ds(r * ROWS + zo * CX, CX)
                    w[v, rows, 0:FULL] = high
                    w[v, rows, FULL:2 * FULL] = (whole - high.astype(F32)).astype(BF)
            scale = 1.0 / jnp.full((8, ny), sums[2], F32)
            for t in range(TAPS):
                value = scale * taps[v, r, 2, t]
                for c, place in ((c_f, moved - (t - RADIUS)), (c_a, moved + (t - RADIUS))):
                    inside = (place >= 0) & (place < ny)
                    c[v, r * TAPS + t] = jnp.where(inside, value, 0.0)
        back = (ny - shift[v]) & (ny - 1)
        for z in range(CZ):
            obs_r[v, z] = pltpu.roll(obs[v, z].astype(F32), back, 1)

    columns = range(ny // 128)
    for c in columns:
        nat[4:12, c, 8:24] = est[:, :, 128 * c:128 * c + 128]

    def assemble(k):
        for c in columns:
            at = slice(128 * c, 128 * c + 128)
            for dz, dx in DIRS:
                first, rows = SPOT[(dz, dx)]
                piece = fields[k, first:first + rows, at].astype(F32)
                z0 = {-1: 0, 0: 4, 1: 12}[dz]
                if dx == 0:
                    nat[z0:z0 + 4, c, 8:24] = piece.reshape(4, 16, 128)
                else:
                    x0 = 4 if dx < 0 else 24
                    for z in range(rows // 4):
                        nat[z0 + z, c, x0:x0 + 4] = piece[4 * z:4 * z + 4]

        def relayout(z, carry):
            for i in range(3):
                for c in columns:
                    u[z, i, :, 128 * c:128 * c + 128] = nat[z, c, pl.ds(4 + i, 8, stride=3), :]
            return carry

        lax.fori_loop(0, 16, relayout, 0, unroll=4)

    sub = lax.broadcasted_iota(jnp.int32, (8, 128), 0)
    low_x = jnp.where(ix == 0, 0.0, 1.0)
    high_x = jnp.where(ix == nx - 1, 0.0, 1.0)
    masks = []
    for at, keep in ((1, low_x), (6, high_x)):
        masks.append(jnp.concatenate([jnp.where(sub == at, keep, 1.0)] * (ny // 128), axis=1))
    y_mask = jnp.where(lax.broadcasted_iota(jnp.int32, (8, 128), 1) == 127, 0.0, 1.0)

    def tv(p):
        @pl.when(iz == 0)
        def _():
            u[3] = u[4]

        @pl.when(iz == nz - 1)
        def _():
            u[12] = u[11]

        def planes(step, below):
            z0 = p + step * (8 - p)
            below = list(below)
            here = [u[z0, i] for i in range(3)]
            for z in range(8 - p):
                after = [u[z0 + z + 1, i] for i in range(3)]
                above = [flux(after[i] - here[i]) for i in range(3)]
                fx = [flux(here[i + 1] - here[i]) * masks[i] for i in range(2)]
                fx.append(flux(pltpu.roll(here[0], 7, 0) - here[2]))
                fx_low = [pltpu.roll(fx[2], 1, 0)] + fx[:2]
                for i in range(3):
                    fy = flux(pltpu.roll(here[i], ny - 1, 1) - here[i])
                    fy = jnp.concatenate([fy[:, :ny - 128], fy[:, ny - 128:] * y_mask], axis=1)
                    total = (above[i] - below[i]) + (fx[i] - fx_low[i]) + (fy - pltpu.roll(fy, 1, 1))
                    u[z0 + z, i] = here[i] + TAU * total
                here, below = after, above
            return tuple(below)

        first = tuple(flux(u[p, i] - u[p - 1, i]) for i in range(3))
        lax.fori_loop(0, 2, planes, first)

    def natural(z, carry):
        for i in range(3):
            for c in columns:
                nat[z, c, pl.ds(4 + i, 8, stride=3), :] = u[z, i, :, 128 * c:128 * c + 128]
        return carry

    def rim(k, carry):
        start(k)

        @pl.when(k == 0)
        def _():
            for load in loads[1:]:
                load.wait()

        prepare(k)
        finish_recv(k)

        @pl.when(k < 2)
        def _():
            assemble(k)
            for p in range(1, PASSES // 2 + 1):
                tv(p)
            lax.fori_loop(4, 12, natural, 0, unroll=4)
            fill(k + 1, lambda z: jnp.concatenate([nat[4 + z, c, 8:24] for c in columns], axis=1))

        return carry

    lax.fori_loop(0, 3, rim, 0)

    def f2d(k):
        field = fields[k]
        return jnp.concatenate([field, field], axis=0)

    def along_y(c, v, j, sign):
        parts = [tmp[r, pl.ds(2 * j, 2)] for r in range(RANK)]
        total = None
        for t in range(TAPS):
            term = c[v, t] * parts[0]
            for r in range(1, RANK):
                term = term + c[v, r * TAPS + t] * parts[r]
            move = (sign * (t - RADIUS)) % ny
            if move:
                term = pltpu.roll(term, move, 2)
            total = term if total is None else total + term
        return total

    def forward(v, carry):
        tmp[...] = jnp.dot(w_f[v], f2d(2), preferred_element_type=F32).reshape(tmp.shape)
        flag = inter[v, ix, iz]

        def ratios(j, carry):
            image = along_y(c_f, v, j, -1)
            img[j] = jnp.where(flag > 0, obs_r[v, j] / (image.reshape(CX, ny) + BACKGROUND), 1.0)
            return carry

        lax.fori_loop(0, CZ, ratios, 0, unroll=2)
        fill(3 + v, lambda z: img[z])
        start(3 + v)
        return carry

    lax.fori_loop(0, VIEWS, forward, 0)
    corr[...] = jnp.zeros(corr.shape, F32)

    def adjoint(v, carry):
        finish_recv(3 + v)
        tmp[...] = jnp.dot(w_a[v], f2d(3 + v), preferred_element_type=F32).reshape(tmp.shape)

        def spread(j, carry):
            corr[j] = corr[j] + along_y(c_a, v, j, 1).reshape(CX, ny)
            return carry

        lax.fori_loop(0, CZ, spread, 0, unroll=2)
        return carry

    lax.fori_loop(0, VIEWS, adjoint, 0)

    def finish(z, carry):
        smoothed = jnp.concatenate([nat[4 + z, c, 8:24] for c in columns], axis=1)
        out[z] = smoothed * corr[z] / VIEWS
        return carry

    lax.fori_loop(0, CZ, finish, 0, unroll=4)

    def sent_all(k, carry):
        finish_send(k)
        return carry

    lax.fori_loop(0, ROUNDS, sent_all, 0)


def local(sizes, estimate, observed, psf_taps, view_shift, intersection):
    cz, cx, ny = estimate.shape
    turned = intersection.transpose(0, 2, 1)
    vmem = pl.BlockSpec(memory_space=pltpu.VMEM)
    hbm = pl.BlockSpec(memory_space=pltpu.HBM)
    dma = pltpu.SemaphoreType.DMA
    return pl.pallas_call(
        functools.partial(kernel, sizes),
        out_shape=jax.ShapeDtypeStruct((cz, cx, ny), F32),
        in_specs=[hbm] * 5,
        out_specs=vmem,
        scratch_shapes=[
            pltpu.VMEM((16, ny // 128, 32, 128), F32),
            pltpu.VMEM((16, 3, 8, ny), F32),
            pltpu.VMEM((2, 32, ny), F32),
            pltpu.VMEM((ROUNDS, FULL, ny), BF),
            pltpu.VMEM((ROUNDS, 2, 32, ny), BF),
            pltpu.VMEM((VIEWS, RANK * ROWS, 2 * FULL), BF),
            pltpu.VMEM((VIEWS, RANK * ROWS, 2 * FULL), BF),
            pltpu.VMEM((VIEWS, RANK * TAPS, 8, ny), F32),
            pltpu.VMEM((VIEWS, RANK * TAPS, 8, ny), F32),
            pltpu.VMEM((VIEWS, cz, cx, ny), F32),
            pltpu.VMEM((RANK, 16, 8, ny), F32),
            pltpu.VMEM((CZ, CX, ny), F32),
            pltpu.VMEM((CZ, CX, ny), F32),
            pltpu.SMEM(psf_taps.shape, F32),
            pltpu.SMEM(view_shift.shape, jnp.int32),
            pltpu.SMEM(turned.shape, jnp.int32),
            pltpu.VMEM(estimate.shape, F32),
            pltpu.VMEM(observed.shape, BF),
            dma((ROUNDS, 8)), dma((ROUNDS, 8)), dma((5,)),
        ],
        compiler_params=pltpu.CompilerParams(
            collective_id=0, has_side_effects=True, vmem_limit_bytes=56 * 1024 * 1024),
        cost_estimate=pl.CostEstimate(flops=10**9, bytes_accessed=10**6, transcendentals=5 * 10**6),
    )(psf_taps, view_shift, turned, estimate, observed)


def solution(mesh):
    from jax.sharding import PartitionSpec as P
    sizes = (mesh.shape["bz"], mesh.shape["bxy"])
    return jax.shard_map(
        functools.partial(local, sizes),
        mesh=mesh,
        in_specs=(P("bz", "bxy", None), P(None, "bz", "bxy", None), P(), P(), P()),
        out_specs=P("bz", "bxy", None),
        check_vma=False,
    )
```
